128 devices in a mesh: frames: 16 (over x, z), codes: 8 (over y, core).
Axes of the slice: x: 4, y: 4, z: 4, core: 2. Of those that a mesh axis runs over, the one named last changes fastest.
Arguments:
- features: bfloat16 [32768, 128], P('frames'), may hold values from -500 to 500
- codebook: bfloat16 [65536, 128], P(('codes', 'frames')), may hold values from -50 to 50
- tile_count: int32 [256, 8], P('frames', 'codes'), may hold values from 1 to 16, as said below
- tile_cols: int32 [256, 8, 16], P('frames', 'codes'), may hold values from 0 to 63, as said below
Outputs:
- quantized: float32 [32768, 128], P(('frames', 'codes'))
- col_log_scale: float32 [65536], P(('codes', 'frames'))
The draws below stay inside these ranges and needn't reach their ends.
Inputs may be any that keep to these rules, and one draw needn't show every extreme that they name: `tile_count`: for every tile row the counts over the 8 blocks sum to 64, and exactly one block of the row has 16. `tile_cols`: the first tile_count entries of a tile row and block are distinct; entries from tile_count on are ignored. Every column tile of the whole is live in some tile row.
All inputs are finite; a program needn't handle non-finite values.
Results may differ from the reference program's by a relative error of at most 0.0009.
Values may be sent and summed in bfloat16 or wider, within the bound.
A program may use at most 128 MiB of HBM per device.

```python
import math
import jax
import jax.numpy as jnp
from jax import lax

E = 128
TILE = 128
CT_DEV = 64
ITERS = 4
CBLOCKS = 8
TPR = 64
LINE_PATCH_PLACE = 16
FTILES = 256
FRAMES = 32768
CODEWORDS = 65536


def pattern(key):
    key_big, key_weight, key_order, key_perm, key_base = jax.random.split(key, 5)
    lanes = jnp.arange(CBLOCKS, dtype=jnp.int32)
    biggest = jax.random.randint(key_big, (FTILES,), 0, CBLOCKS, dtype=jnp.int32)
    flagged_selector = lanes[None, :] == biggest[:, None]
    weights = jnp.where(flagged_selector, 0, jax.random.randint(key_weight, (FTILES, CBLOCKS), 1, 3, dtype=jnp.int32))
    spare = TPR - LINE_PATCH_PLACE - (CBLOCKS - 1)
    additional_number = spare * weights // jnp.sum(weights, axis=1, keepdims=True)
    remainder_number = spare - jnp.sum(additional_number, axis=1, keepdims=True)
    order_keys = jax.random.randint(key_order, (FTILES, CBLOCKS), 0, 1 << 20, dtype=jnp.int32) * CBLOCKS + lanes[None, :]
    order_keys = jnp.where(flagged_selector, (1 << 20) * CBLOCKS + lanes[None, :], order_keys)
    ordinal_position = jnp.argsort(jnp.argsort(order_keys, axis=1), axis=1).astype(jnp.int32)
    surplus_quantity = (ordinal_position < remainder_number).astype(jnp.int32)
    tally_aggregate = jnp.where(flagged_selector, LINE_PATCH_PLACE, 1 + additional_number + surplus_quantity).astype(jnp.int32)
    bases = jax.random.randint(key_base, (1, CBLOCKS), 0, CT_DEV, dtype=jnp.int32)
    starts = jnp.cumsum(tally_aggregate, axis=0, dtype=jnp.int32) - tally_aggregate + bases
    perm_keys = jax.random.split(key_perm, CBLOCKS)
    perms = jax.vmap(lambda one_key: jax.random.permutation(one_key, CT_DEV))(perm_keys).astype(jnp.int32)
    positions = (starts[:, :, None] + jnp.arange(LINE_PATCH_PLACE, dtype=jnp.int32)[None, None, :]) % CT_DEV
    chosen = perms[lanes[None, :, None], positions].astype(jnp.int32)
    return (tally_aggregate, chosen)


def shared_basis(key):
    key = jax.random.fold_in(key, 29)
    key_dirs, key_comp = jax.random.split(key)
    directions = jnp.clip(jax.random.normal(key_dirs, (8, E), jnp.float32), -3.0, 3.0)
    components = jnp.exp(jax.random.uniform(key_comp, (1, E), jnp.float32, 0.0, math.log(10.0)))
    return (directions, components)


def draw_tile_count(key, part):
    return pattern(key)[0]


def draw_tile_cols(key, part):
    return pattern(key)[1]


def draw_features(key, part):
    directions, components = shared_basis(key)
    key = jax.random.fold_in(key, 11)
    key_base, key_rows, key_pick = jax.random.split(key, 3)
    picks = jax.random.randint(key_pick, (3, FRAMES), 0, 8, dtype=jnp.int32)
    cluster = jnp.min(picks, axis=0)
    centre = jnp.take(directions, cluster, axis=0)
    row_scale = jnp.exp(jax.random.uniform(key_rows, (FRAMES, 1), jnp.float32, 0.0, math.log(10.0)))
    base = centre + 0.5 * jnp.clip(jax.random.normal(key_base, (FRAMES, E), jnp.float32), -4.0, 4.0)
    return (base * components * row_scale).astype(jnp.bfloat16)


def draw_codebook(key, part):
    directions, components = shared_basis(key)
    key = jax.random.fold_in(key, 13)
    key_base, key_rows, key_pick = jax.random.split(key, 3)
    cluster = jax.random.randint(key_pick, (CODEWORDS,), 0, 8, dtype=jnp.int32)
    centre = jnp.take(directions, cluster, axis=0)
    row_scale = jnp.exp(jax.random.uniform(key_rows, (CODEWORDS, 1), jnp.float32, math.log(0.3), math.log(3.0)))
    base = centre + 0.6 * jnp.clip(jax.random.normal(key_base, (CODEWORDS, E), jnp.float32), -4.0, 4.0)
    return (base * (0.3 * components) * row_scale).astype(jnp.bfloat16)


def setup_inputs(seed: int = 0) -> dict:
    seeds = jax.random.split(jax.random.key(seed), 5)
    return {
        "features": draw_features(jax.random.fold_in(seeds[4], 71), 0),
        "codebook": draw_codebook(jax.random.fold_in(seeds[4], 71), 0),
        "tile_count": draw_tile_count(jax.random.fold_in(seeds[4], 71), 0),
        "tile_cols": draw_tile_cols(jax.random.fold_in(seeds[4], 71), 0),
    }


EPS = 1e-06
INV_TEMP = 10.0

def reference(features, codebook, tile_count, tile_cols):
    high = lax.Precision.HIGHEST
    feat_scale = lax.rsqrt(lax.optimization_barrier(jnp.mean(jnp.square(features.astype(jnp.float32)), axis=-1)) + EPS).reshape(FTILES, TILE)
    code_scale = lax.rsqrt(lax.optimization_barrier(jnp.mean(jnp.square(codebook.astype(jnp.float32)), axis=-1)) + EPS).reshape(CBLOCKS * CT_DEV, TILE)
    book_tiles = codebook.reshape(CBLOCKS * CT_DEV, TILE, E)
    feat_tiles = features.reshape(FTILES, TILE, E)
    offsets = (jnp.arange(CBLOCKS, dtype=jnp.int32) * CT_DEV)[None, :, None]
    global_cols = (tile_cols.astype(jnp.int32) + offsets).reshape(FTILES, CBLOCKS * LINE_PATCH_PLACE)
    slot_live = (jnp.arange(LINE_PATCH_PLACE, dtype=jnp.int32)[None, None, :] < tile_count[:, :, None]).astype(jnp.float32)
    slot_live = slot_live.reshape(FTILES, CBLOCKS * LINE_PATCH_PLACE)
    row_index = jnp.arange(FTILES, dtype=jnp.int32)

    def kernel_row(index):
        chosen = global_cols[index]
        picked = jnp.take(book_tiles, chosen, axis=0)
        products = jnp.einsum('fe,ske->sfk', feat_tiles[index].astype(jnp.float32), picked.astype(jnp.float32), precision=high)
        scaled = INV_TEMP / E * products * feat_scale[index][None, :, None] * jnp.take(code_scale, chosen, axis=0)[:, None, :]
        return (jnp.exp(scaled) * slot_live[index][:, None, None], chosen, picked)

    def half_kernel(index):
        kernel, chosen, picked = kernel_row(index)
        kernel_half = lax.optimization_barrier(kernel.astype(jnp.bfloat16))
        return (kernel_half.astype(jnp.float32), chosen)
    target = FRAMES / CODEWORDS
    v_tiles = jnp.ones((CBLOCKS * CT_DEV, TILE), jnp.float32)
    u_tiles = jnp.ones((FTILES, TILE), jnp.float32)
    for sweep in range(ITERS):
        v_half = lax.optimization_barrier(v_tiles.astype(jnp.bfloat16)).astype(jnp.float32)

        def row_part(index):
            kernel, chosen = half_kernel(index)
            return jnp.einsum('sfk,sk->f', kernel, jnp.take(v_half, chosen, axis=0), precision=high)
        u_tiles = 1.0 / lax.map(row_part, row_index)
        u_half = lax.optimization_barrier(u_tiles.astype(jnp.bfloat16)).astype(jnp.float32)

        def col_part(carry, index):
            kernel, chosen = half_kernel(index)
            contrib = jnp.einsum('sfk,f->sk', kernel, u_half[index], precision=high)
            return (carry.at[chosen].add(contrib), None)
        col_tiles, unused = lax.scan(col_part, jnp.zeros((CBLOCKS * CT_DEV, TILE), jnp.float32), row_index)
        v_tiles = target / col_tiles

    def mix_row(index):
        kernel, chosen, picked = kernel_row(index)
        weights = (kernel * jnp.take(v_tiles, chosen, axis=0)[:, None, :]).astype(jnp.bfloat16)
        mixed = jnp.einsum('sfk,ske->fe', weights.astype(jnp.float32), picked.astype(jnp.float32), precision=high)
        return u_tiles[index][:, None] * mixed
    quantized = lax.map(mix_row, row_index).reshape(FRAMES, E)
    return (quantized, jnp.log(v_tiles.reshape(CODEWORDS)))
```

```python
import functools
import math

import jax
import jax.numpy as jnp
from jax import lax
from jax.experimental import pallas as pl
from jax.experimental.pallas import tpu as pltpu
from jax.sharding import PartitionSpec as P

ITERS = 4
EPS = 1e-06
INV_TEMP = 10.0
TILE = 128
SLOTS = 16
ROWS = 16
NF = 16
NC = 8
OWN = 4
PAD = 8
F32 = jnp.float32
BF16 = jnp.bfloat16
NT = (((1,), (1,)), ((), ()))
MESH = pl.DeviceIdType.MESH
FAR = sorted(
    ((a, b) for a in range(4) for b in range(4) if (a, b) != (0, 0)),
    key=lambda d: -min(d[0], 4 - d[0]) - min(d[1], 4 - d[1]))


def tile_rows(i):
    return pl.ds(pl.multiple_of(i * TILE, TILE), TILE)


def share(p):
    return pl.ds(pl.multiple_of(p * PAD, PAD), PAD)


def column(row):
    return jnp.broadcast_to(row, (TILE, TILE)).T


def kernel(target, feat_hbm, code_hbm, cnt_s, cols_s, cols_hbm, q_out, log_out,
           feat, cols_v, book, K, fs, cs, pick, place, contrib, rowrx, colb, colf, v_ref, u_ref,
           tosib, fromsib, mine, yrx,
           feat_sem, cols_sem, code_sem, book_s, book_r, cs_s, cs_r, row_s, row_r, col_s, col_r,
           sib_s, sib_r, y_s, y_r):
    me_f = lax.axis_index("frames")
    me_c = lax.axis_index("codes")
    x, z = me_f // 4, lax.rem(me_f, 4)
    y, core = me_c // 2, lax.rem(me_c, 2)
    sub16 = lax.broadcasted_iota(jnp.int32, (ROWS, TILE), 0)
    lane16 = lax.broadcasted_iota(jnp.int32, (ROWS, TILE), 1)

    def peer_f(k):
        return lax.rem(me_f + k, NF)

    def peer_c(k):
        return lax.rem(me_c + k, NC)

    def send(src, dst, ss, rs, where):
        pltpu.make_async_remote_copy(
            src_ref=src, dst_ref=dst, send_sem=ss, recv_sem=rs,
            device_id=where, device_id_type=MESH,
        ).start()

    def drain(ref, sem):
        pltpu.make_async_copy(ref, ref, sem).wait()

    own_book = book.at[pl.ds(me_f * OWN, OWN)]
    code_copy = pltpu.make_async_copy(code_hbm, own_book, code_sem)
    code_copy.start()
    feat_copy = pltpu.make_async_copy(feat_hbm, feat, feat_sem)
    feat_copy.start()
    cols_copy = pltpu.make_async_copy(cols_hbm, cols_v, cols_sem)
    cols_copy.start()

    barrier = pltpu.get_barrier_semaphore()
    for k in range(1, NF):
        pl.semaphore_signal(barrier, inc=1, device_id={"frames": peer_f(k)}, device_id_type=MESH)
    for k in range(1, NC):
        pl.semaphore_signal(barrier, inc=1, device_id={"codes": peer_c(k)}, device_id_type=MESH)
    pl.semaphore_wait(barrier, NF - 1 + NC - 1)
    code_copy.wait()

    def at(h, first, second):
        dx, dz = (first, second) if h == 0 else (second, first)
        return lax.rem(x + dx, 4) * 4 + lax.rem(z + dz, 4)

    def chunk(h, first, second, q=None):
        base = at(h, first, second) * OWN + 2 * h
        return book.at[pl.ds(base, 2)] if q is None else book.at[pl.ds(base + q, 1)]

    def pass_on(h, stage, way, ref, first, second):
        send(ref, ref, book_s, book_r.at[h, stage, way], {"frames": at(h, first, second)})

    def first_sends(h):
        pass_on(h, 0, 0, chunk(h, 0, 0), 1, 0)
        pass_on(h, 0, 1, chunk(h, 0, 0), 3, 0)

    def first_forwards(h):
        drain(chunk(h, 3, 0), book_r.at[h, 0, 0])
        pass_on(h, 1, 0, chunk(h, 3, 0, 0), 1, 0)
        drain(chunk(h, 1, 0), book_r.at[h, 0, 1])
        pass_on(h, 1, 1, chunk(h, 1, 0, 1), 3, 0)

    def second_sends(h, j):
        pass_on(h, 2 + j, 0, chunk(h, j, 0), 0, 1)
        pass_on(h, 2 + j, 1, chunk(h, j, 0), 0, 3)

    def second_forwards(h, j):
        drain(chunk(h, j, 3), book_r.at[h, 2 + j, 0])
        pass_on(h, 6 + j, 0, chunk(h, j, 3, 0), 0, 1)
        drain(chunk(h, j, 1), book_r.at[h, 2 + j, 1])
        pass_on(h, 6 + j, 1, chunk(h, j, 1, 1), 0, 3)

    for h in range(2):
        first_sends(h)
    for h in range(2):
        second_sends(h, 0)

    scales = []
    for t in range(OWN):
        own = book[me_f * OWN + t].astype(F32)
        scales.append(lax.rsqrt(jnp.sum((own * own).T, axis=0, keepdims=True) / TILE + EPS))
    cs[share(me_f), :] = jnp.concatenate(scales + [jnp.ones((PAD - OWN, TILE), F32)], axis=0)
    for k in range(1, NF):
        send(cs.at[share(me_f)], cs.at[share(me_f)], cs_s, cs_r, {"frames": peer_f(k)})

    for h in range(2):
        first_forwards(h)
    for h in range(2):
        second_sends(h, 1)
        second_sends(h, 3)
    for h in range(2):
        second_forwards(h, 0)
    for h in range(2):
        drain(chunk(h, 2, 0, 0), book_r.at[h, 1, 0])
        drain(chunk(h, 2, 0, 1), book_r.at[h, 1, 1])
        second_sends(h, 2)

    feat_copy.wait()
    cols_copy.wait()

    def frame_scale(i, _):
        part = feat[tile_rows(i), :].astype(F32)
        m = jnp.sum(part * part, axis=1, keepdims=True) / TILE
        s = lax.rsqrt(m + EPS) * (INV_TEMP / TILE * math.log2(math.e))
        fs[tile_rows(i), :] = jnp.broadcast_to(s, (TILE, TILE))
        return 0

    lax.fori_loop(0, ROWS, frame_scale, 0)
    for h in range(2):
        second_forwards(h, 1)
        second_forwards(h, 3)

    count = jnp.zeros((ROWS, SLOTS), jnp.int32)
    for i in range(ROWS):
        count = jnp.where(lax.broadcasted_iota(jnp.int32, count.shape, 0) == i, cnt_s[0, i], count)
    cv = jnp.where(lax.broadcasted_iota(jnp.int32, count.shape, 1) < count, cols_v[:, 0, :], -1)
    for s in range(SLOTS):
        hot = (jnp.broadcast_to(cv[:, s:s + 1], (ROWS, TILE)) == lane16).astype(F32)
        pick[s * ROWS:(s + 1) * ROWS, :] = hot[:, :NF * OWN].astype(BF16)
        contrib[s * ROWS:(s + 1) * ROWS, :] = hot
    for h in range(2):
        turned = contrib[h * TILE:(h + 1) * TILE, :].T[:NF * OWN].astype(BF16)
        for j in range(3):
            place[:, j * 2 * TILE + h * TILE:j * 2 * TILE + (h + 1) * TILE] = turned

    for h in range(2):
        second_forwards(h, 2)
    for h in range(2):
        for j in range(4):
            drain(chunk(h, j, 2, 0), book_r.at[h, 6 + j, 0])
            drain(chunk(h, j, 2, 1), book_r.at[h, 6 + j, 1])
    drain(cs.at[pl.ds(0, (NF - 1) * PAD)], cs_r)

    def build(i, _):
        a = feat[tile_rows(i), :]
        f = fs[tile_rows(i), :]
        f = jnp.concatenate([f, f], axis=1)
        for s in range(0, SLOTS, 2):
            at2 = [cols_s[i, 0, s + j] for j in range(2)]
            words = jnp.concatenate([book[c] for c in at2], axis=0)
            scale = jnp.concatenate(
                [cs[pl.ds((c // OWN) * PAD + lax.rem(c, OWN), 1), :] for c in at2], axis=1)
            p = lax.dot_general(a, words, NT, preferred_element_type=F32)
            K[tile_rows(i), s * TILE:(s + 2) * TILE] = jnp.exp2(p * f * scale).astype(BF16)
        return 0

    lax.fori_loop(0, ROWS, build, 0, unroll=2)

    v_ref[...] = jnp.ones_like(v_ref)

    def sweep(it, last):
        chosen = jnp.dot(pick[...], v_ref[...].astype(BF16), preferred_element_type=F32).astype(BF16)
        V = jnp.concatenate([chosen[s * ROWS:(s + 1) * ROWS, :] for s in range(SLOTS)], axis=1)

        r = lax.dot_general(V, K[...], NT, preferred_element_type=F32)
        sums = r[:, :TILE]
        for i in range(1, ROWS):
            sums = jnp.where(sub16 == i, r[:, i * TILE:(i + 1) * TILE], sums)
        rowrx[it, me_c] = sums
        for dy, dk in ((2, 1), (2, 0), (1, 1), (3, 1), (1, 0), (3, 0), (0, 1)):
            send(rowrx.at[it, me_c], rowrx.at[it, me_c], row_s.at[it], row_r.at[it],
                 {"codes": lax.rem(y + dy, 4) * 2 + lax.rem(core + dk, 2)})
        drain(rowrx.at[it, pl.ds(0, NC - 1)], row_r.at[it])
        total = rowrx[it, 0]
        for c in range(1, NC):
            total = total + rowrx[it, c]
        u = 1.0 / total
        u_ref[...] = u
        U = jnp.concatenate([jnp.where(sub16 == i, u, 0.0) for i in range(ROWS)], axis=1).astype(BF16)

        r = jnp.dot(U, K[...], preferred_element_type=F32)
        rest = jnp.concatenate([r[:, s * TILE:(s + 1) * TILE] for s in range(SLOTS)], axis=0)
        hi = rest.astype(BF16)
        rest = rest - hi.astype(F32)
        mid = rest.astype(BF16)
        lo = (rest - mid.astype(F32)).astype(BF16)
        cols = jnp.dot(place[...], jnp.concatenate([hi, mid, lo], axis=0), preferred_element_type=F32)
        got = colf if last else colb.at[it]
        got[me_f] = cols.astype(got.dtype)
        for dx, dz in FAR:
            send(got.at[me_f], got.at[me_f], col_s.at[it], col_r.at[it], {"frames": at(0, dx, dz)})
        drain(got.at[pl.ds(0, NF - 1)], col_r.at[it])
        csum = got[0].astype(F32)
        for p in range(1, NF):
            csum = csum + got[p].astype(F32)
        v_ref[...] = target / csum

    def early(it, _):
        sweep(it, False)
        return 0

    lax.fori_loop(0, ITERS - 1, early, 0)
    sweep(ITERS - 1, True)
    log_out[...] = jnp.log(jnp.concatenate(
        [v_ref[pl.ds(me_f * OWN + t, 1), :] for t in range(OWN)], axis=0))

    def mix(c, dst):
        def one(j, _):
            i = 2 * c + j
            n = cnt_s[0, i]
            weights, words = [], []
            for s in range(SLOTS):
                word = cols_s[i, 0, s]
                scale = v_ref[pl.ds(word, 1), :] * jnp.where(s < n, 1.0, 0.0)
                k = K[tile_rows(i), s * TILE:(s + 1) * TILE].astype(F32)
                weights.append((k * scale).astype(BF16))
                words.append(book[word])
            dst[tile_rows(j), :] = jnp.dot(
                jnp.concatenate(weights, axis=1), jnp.concatenate(words, axis=0),
                preferred_element_type=F32)
            return 0

        lax.fori_loop(0, 2, one, 0)

    def chip(k):
        return lax.rem(y + 2 + k * (k + 1) // 2, 4)

    def join(k):
        drain(fromsib.at[k], sib_r.at[k])
        mine[k] = mine[k] + fromsib[k]

    def forward(k):
        join(k)
        send(mine.at[k], yrx.at[k], y_s.at[k], y_r.at[k], {"codes": chip(k) * 2 + core})

    def mix_step(k, _):
        mix(chip(k) * 2 + 1 - core, tosib.at[k])
        send(tosib.at[k], fromsib.at[k], sib_s.at[k], sib_r.at[k], {"codes": y * 2 + 1 - core})
        mix(chip(k) * 2 + core, mine.at[k])

        @pl.when(k > 0)
        def _():
            forward(k - 1)

        return 0

    lax.fori_loop(0, 4, mix_step, 0)
    join(3)
    for k in range(3):
        drain(yrx.at[k], y_r.at[k])
    for j in range(2):
        rows = slice(j * TILE, (j + 1) * TILE)
        acc = mine[3, rows, :]
        for k in range(3):
            acc = acc + yrx[k, rows, :]
        q_out[rows, :] = acc * column(u_ref[pl.ds(2 * me_c + j, 1), :])

    drain(book.at[pl.ds(0, 60)], book_s)
    drain(cs.at[pl.ds(0, (NF - 1) * PAD)], cs_s)
    for it in range(ITERS):
        drain(rowrx.at[it, pl.ds(0, NC - 1)], row_s.at[it])
        got = colf if it == ITERS - 1 else colb.at[it]
        drain(got.at[pl.ds(0, NF - 1)], col_s.at[it])
    for k in range(4):
        drain(tosib.at[k], sib_s.at[k])
    for k in range(3):
        drain(mine.at[k], y_s.at[k])


def per_device(target, features, codebook, tile_count, tile_cols):
    vmem = pl.BlockSpec(memory_space=pltpu.VMEM)
    smem = pl.BlockSpec(memory_space=pltpu.SMEM)
    hbm = pl.BlockSpec(memory_space=pl.ANY)
    dma = pltpu.SemaphoreType.DMA
    quantized, logs = pl.pallas_call(
        functools.partial(kernel, target),
        out_shape=(
            jax.ShapeDtypeStruct((2 * TILE, TILE), F32),
            jax.ShapeDtypeStruct((OWN, TILE), F32),
        ),
        in_specs=[hbm, hbm, smem, smem, hbm],
        out_specs=(vmem, vmem),
        scratch_shapes=[
            pltpu.VMEM((ROWS * TILE, TILE), BF16),
            pltpu.VMEM((ROWS, 1, SLOTS), jnp.int32),
            pltpu.VMEM((NF * OWN, TILE, TILE), BF16),
            pltpu.VMEM((ROWS * TILE, SLOTS * TILE), BF16),
            pltpu.VMEM((ROWS * TILE, TILE), F32),
            pltpu.VMEM((NF * PAD, TILE), F32),
            pltpu.VMEM((SLOTS * ROWS, NF * OWN), BF16),
            pltpu.VMEM((NF * OWN, 3 * SLOTS * ROWS), BF16),
            pltpu.VMEM((SLOTS * ROWS, TILE), F32),
            pltpu.VMEM((ITERS, NC, ROWS, TILE), F32),
            pltpu.VMEM((ITERS - 1, NF, NF * OWN, TILE), BF16),
            pltpu.VMEM((NF, NF * OWN, TILE), F32),
            pltpu.VMEM((NF * OWN, TILE), F32),
            pltpu.VMEM((ROWS, TILE), F32),
            pltpu.VMEM((4, 2 * TILE, TILE), F32),
            pltpu.VMEM((4, 2 * TILE, TILE), F32),
            pltpu.VMEM((4, 2 * TILE, TILE), F32),
            pltpu.VMEM((3, 2 * TILE, TILE), F32),
            dma, dma, dma, dma, dma((2, 10, 2)), dma, dma,
            dma((ITERS,)), dma((ITERS,)), dma((ITERS,)), dma((ITERS,)),
            dma((4,)), dma((4,)), dma((4,)), dma((4,)),
        ],
        compiler_params=pltpu.CompilerParams(
            collective_id=0, has_side_effects=True, vmem_limit_bytes=60 * 2**20),
    )(features, codebook.reshape(OWN, TILE, TILE), tile_count.reshape(1, ROWS), tile_cols, tile_cols)
    return quantized, logs.reshape(OWN * TILE)


def solution(mesh):
    target = 32768 / 65536
    return jax.shard_map(
        functools.partial(per_device, target),
        mesh=mesh,
        in_specs=(
            P("frames", None),
            P(("codes", "frames"), None),
            P("frames", "codes"),
            P("frames", "codes", None),
        ),
        out_specs=(P(("frames", "codes"), None), P(("codes", "frames"))),
        check_vma=False,
    )
```

```python
import functools
import math

import jax
import jax.numpy as jnp
from jax import lax
from jax.experimental import pallas as pl
from jax.experimental.pallas import tpu as pltpu
from jax.sharding import PartitionSpec as P

ITERS = 4
EPS = 1e-06
INV_TEMP = 10.0
TILE = 128
SLOTS = 16
ROWS = 16
NF = 16
NC = 8
SPLIT = 5
HALF = 32
OWN = 4
PAD = 8
F32 = jnp.float32
BF16 = jnp.bfloat16
NT = (((1,), (1,)), ((), ()))
MESH = pl.DeviceIdType.MESH


def tile_rows(i):
    return pl.ds(pl.multiple_of(i * TILE, TILE), TILE)


def share(p):
    return pl.ds(pl.multiple_of(p * PAD, PAD), PAD)


def column(row):
    return jnp.broadcast_to(row, (TILE, TILE)).T


def kernel(target, feat_hbm, code_hbm, cnt_s, cols_s, cols_hbm, q_out, log_out,
           feat, cols_v, book, K, exact, fs, cs, pick, place, contrib, rowrx, sums, v_ref, u_ref,
           tosib, fromsib, mine, yrx,
           feat_sem, cols_sem, code_sem, book_s, book_r, cs_s, cs_r, row_s, row_r, col_s, col_r,
           sib_s, sib_r, y_s, y_r):
    me_f = lax.axis_index("frames")
    me_c = lax.axis_index("codes")
    x, z = me_f // 4, lax.rem(me_f, 4)
    y, core = me_c // 2, lax.rem(me_c, 2)
    sub16 = lax.broadcasted_iota(jnp.int32, (ROWS, TILE), 0)
    lane = lax.broadcasted_iota(jnp.int32, (TILE, TILE), 1)
    sub8 = lax.broadcasted_iota(jnp.int32, (8, TILE), 0)
    lane16 = lax.broadcasted_iota(jnp.int32, (ROWS, TILE), 1)

    def peer_f(k):
        return lax.rem(me_f + k, NF)

    def peer_c(k):
        return lax.rem(me_c + k, NC)

    def send(src, dst, ss, rs, where):
        pltpu.make_async_remote_copy(
            src_ref=src, dst_ref=dst, send_sem=ss, recv_sem=rs,
            device_id=where, device_id_type=MESH,
        ).start()

    def drain(ref, sem):
        pltpu.make_async_copy(ref, ref, sem).wait()

    own_book = book.at[pl.ds(me_f * OWN, OWN)]
    code_copy = pltpu.make_async_copy(code_hbm, own_book, code_sem)
    code_copy.start()
    feat_copy = pltpu.make_async_copy(feat_hbm, feat, feat_sem)
    feat_copy.start()
    cols_copy = pltpu.make_async_copy(cols_hbm, cols_v, cols_sem)
    cols_copy.start()

    barrier = pltpu.get_barrier_semaphore()
    for k in range(1, NF):
        pl.semaphore_signal(barrier, inc=1, device_id={"frames": peer_f(k)}, device_id_type=MESH)
    for k in range(1, NC):
        pl.semaphore_signal(barrier, inc=1, device_id={"codes": peer_c(k)}, device_id_type=MESH)
    pl.semaphore_wait(barrier, NF - 1 + NC - 1)
    code_copy.wait()

    def at(h, first, second):
        dx, dz = (first, second) if h == 0 else (second, first)
        return lax.rem(x + dx, 4) * 4 + lax.rem(z + dz, 4)

    def chunk(h, first, second, q=None):
        base = at(h, first, second) * OWN + 2 * h
        return book.at[pl.ds(base, 2)] if q is None else book.at[pl.ds(base + q, 1)]

    def pass_on(h, stage, way, ref, first, second):
        send(ref, ref, book_s, book_r.at[h, stage, way], {"frames": at(h, first, second)})

    def first_sends(h):
        pass_on(h, 0, 0, chunk(h, 0, 0), 1, 0)
        pass_on(h, 0, 1, chunk(h, 0, 0), 3, 0)

    def first_forwards(h):
        drain(chunk(h, 3, 0), book_r.at[h, 0, 0])
        pass_on(h, 1, 0, chunk(h, 3, 0, 0), 1, 0)
        drain(chunk(h, 1, 0), book_r.at[h, 0, 1])
        pass_on(h, 1, 1, chunk(h, 1, 0, 1), 3, 0)

    def second_sends(h, j):
        pass_on(h, 2 + j, 0, chunk(h, j, 0), 0, 1)
        pass_on(h, 2 + j, 1, chunk(h, j, 0), 0, 3)

    def second_forwards(h, j):
        drain(chunk(h, j, 3), book_r.at[h, 2 + j, 0])
        pass_on(h, 6 + j, 0, chunk(h, j, 3, 0), 0, 1)
        drain(chunk(h, j, 1), book_r.at[h, 2 + j, 1])
        pass_on(h, 6 + j, 1, chunk(h, j, 1, 1), 0, 3)

    for h in range(2):
        first_sends(h)
    for h in range(2):
        second_sends(h, 0)

    scales = []
    for t in range(OWN):
        own = book[me_f * OWN + t].astype(F32)
        scales.append(lax.rsqrt(jnp.sum((own * own).T, axis=0, keepdims=True) / TILE + EPS))
    cs[share(me_f), :] = jnp.concatenate(scales + [jnp.ones((PAD - OWN, TILE), F32)], axis=0)
    for k in range(1, NF):
        send(cs.at[share(me_f)], cs.at[share(me_f)], cs_s, cs_r, {"frames": peer_f(k)})

    for h in range(2):
        first_forwards(h)
    for h in range(2):
        second_sends(h, 1)
        second_sends(h, 3)
    for h in range(2):
        second_forwards(h, 0)
    for h in range(2):
        drain(chunk(h, 2, 0, 0), book_r.at[h, 1, 0])
        drain(chunk(h, 2, 0, 1), book_r.at[h, 1, 1])
        second_sends(h, 2)

    feat_copy.wait()
    cols_copy.wait()

    def frame_scale(i, _):
        part = feat[tile_rows(i), :].astype(F32)
        m = jnp.sum(part * part, axis=1, keepdims=True) / TILE
        s = lax.rsqrt(m + EPS) * (INV_TEMP / TILE * math.log2(math.e))
        fs[tile_rows(i), :] = jnp.broadcast_to(s, (TILE, TILE))
        return 0

    lax.fori_loop(0, ROWS, frame_scale, 0)
    for h in range(2):
        second_forwards(h, 1)
        second_forwards(h, 3)

    count = jnp.zeros((ROWS, SLOTS), jnp.int32)
    for i in range(ROWS):
        count = jnp.where(lax.broadcasted_iota(jnp.int32, count.shape, 0) == i, cnt_s[0, i], count)
    cv = jnp.where(lax.broadcasted_iota(jnp.int32, count.shape, 1) < count, cols_v[:, 0, :], -1)
    for s in range(SLOTS):
        hot = (jnp.broadcast_to(cv[:, s:s + 1], (ROWS, TILE)) == lane16).astype(F32)
        pick[s * ROWS:(s + 1) * ROWS, :] = hot[:, :NF * OWN].astype(BF16)
        contrib[s * ROWS:(s + 1) * ROWS, :] = hot
    for h in range(2):
        turned = contrib[h * TILE:(h + 1) * TILE, :].T[:NF * OWN].astype(BF16)
        for j in range(3):
            place[:, j * 2 * TILE + h * TILE:j * 2 * TILE + (h + 1) * TILE] = turned

    for h in range(2):
        second_forwards(h, 2)
    for h in range(2):
        for j in range(4):
            drain(chunk(h, j, 2, 0), book_r.at[h, 6 + j, 0])
            drain(chunk(h, j, 2, 1), book_r.at[h, 6 + j, 1])
    drain(cs.at[pl.ds(0, (NF - 1) * PAD)], cs_r)

    def build(i, _):
        a = feat[tile_rows(i), :]
        f = fs[tile_rows(i), :]
        f = jnp.concatenate([f, f], axis=1)
        for s in range(0, SLOTS, 2):
            at2 = [cols_s[i, 0, s + j] for j in range(2)]
            words = jnp.concatenate([book[c] for c in at2], axis=0)
            scale = jnp.concatenate(
                [cs[pl.ds((c // OWN) * PAD + lax.rem(c, OWN), 1), :] for c in at2], axis=1)
            p = lax.dot_general(a, words, NT, preferred_element_type=F32)
            k = jnp.exp2(p * f * scale)
            exact[tile_rows(i), s * TILE:(s + 2) * TILE] = k
            K[tile_rows(i), s * TILE:(s + 2) * TILE] = k.astype(BF16)
        return 0

    lax.fori_loop(0, ROWS, build, 0, unroll=2)

    v_ref[...] = jnp.ones_like(v_ref)

    def hop(it, stage, h, values):
        along_x = stage == h
        slot = sums.at[it, stage, h, x if along_x else z]
        slot[...] = values
        for k in (2, 1, 3):
            where = at(0, k, 0) if along_x else at(0, 0, k)
            send(slot, slot, col_s.at[it, stage, h], col_r.at[it, stage, h], {"frames": where})

    def gathered(it, stage, h):
        drain(sums.at[it, stage, h, pl.ds(0, 3)], col_r.at[it, stage, h])
        return (sums[it, stage, h, 0] + sums[it, stage, h, 1]) + (sums[it, stage, h, 2] + sums[it, stage, h, 3])

    def sweep(it, _):
        contrib[...] = jnp.dot(pick[...], v_ref[...].astype(BF16), preferred_element_type=F32)
        V = jnp.concatenate(
            [contrib[s * ROWS:(s + 1) * ROWS, :] for s in range(SPLIT)], axis=1).astype(BF16)

        r = lax.dot_general(V, K[:, :SPLIT * TILE], NT, preferred_element_type=F32)
        side = jnp.zeros((TILE, TILE), F32)
        for g in range(2):
            for i in range(g * 8, g * 8 + 8):
                acc = jnp.zeros((TILE, TILE), F32)
                for s in range(SPLIT, SLOTS):
                    k = K[i * TILE:(i + 1) * TILE, s * TILE:(s + 1) * TILE].astype(F32)
                    acc = acc + k * contrib[s * ROWS + i:s * ROWS + i + 1, :]
                side = jnp.where(lane == i, jnp.sum(acc, axis=1, keepdims=True), side)
            total = side.T[g * 8:g * 8 + 8]
            for i in range(g * 8, g * 8 + 8):
                total = total + jnp.where(
                    sub8 == i - g * 8, r[g * 8:g * 8 + 8, i * TILE:(i + 1) * TILE], 0.0)
            slot = rowrx.at[it, g, me_c]
            slot[...] = total
            for dy, dk in ((2, 1), (2, 0), (1, 1), (3, 1), (1, 0), (3, 0), (0, 1)):
                send(slot, slot, row_s.at[it, g], row_r.at[it, g],
                     {"codes": lax.rem(y + dy, 4) * 2 + lax.rem(core + dk, 2)})
        parts = []
        for g in range(2):
            drain(rowrx.at[it, g, pl.ds(0, NC - 1)], row_r.at[it, g])
            total = rowrx[it, g, 0]
            for c in range(1, NC):
                total = total + rowrx[it, g, c]
            u = 1.0 / total
            u_ref[g * 8:g * 8 + 8, :] = u
            U = jnp.concatenate(
                [jnp.where(sub8 == i, u, 0.0) for i in range(8)], axis=1).astype(BF16)
            parts.append(jnp.dot(U, K[g * 8 * TILE:(g + 1) * 8 * TILE, :], preferred_element_type=F32))
        rest = jnp.concatenate(
            [parts[g][:, s * TILE:(s + 1) * TILE] for s in range(SLOTS) for g in range(2)], axis=0)
        hi = rest.astype(BF16)
        rest = rest - hi.astype(F32)
        mid = rest.astype(BF16)
        lo = (rest - mid.astype(F32)).astype(BF16)
        cols = jnp.dot(place[...], jnp.concatenate([hi, mid, lo], axis=0), preferred_element_type=F32)
        for h in range(2):
            hop(it, 0, h, cols[h * HALF:(h + 1) * HALF])
        for h in range(2):
            hop(it, 1, h, gathered(it, 0, h))
        csum = jnp.concatenate([gathered(it, 1, h) for h in range(2)], axis=0)
        v_ref[...] = target / csum
        return 0

    lax.fori_loop(0, ITERS, sweep, 0)
    log_out[...] = jnp.log(jnp.concatenate(
        [v_ref[pl.ds(me_f * OWN + t, 1), :] for t in range(OWN)], axis=0))

    def mix(c, dst):
        def one(j, _):
            i = 2 * c + j
            n = cnt_s[0, i]
            weights, words = [], []
            for s in range(SLOTS):
                word = cols_s[i, 0, s]
                scale = v_ref[pl.ds(word, 1), :] * jnp.where(s < n, 1.0, 0.0)
                k = exact[tile_rows(i), s * TILE:(s + 1) * TILE]
                weights.append((k * scale).astype(BF16))
                words.append(book[word])
            dst[tile_rows(j), :] = jnp.dot(
                jnp.concatenate(weights, axis=1), jnp.concatenate(words, axis=0),
                preferred_element_type=F32)
            return 0

        lax.fori_loop(0, 2, one, 0)

    def chip(k):
        return lax.rem(y + 2 + k * (k + 1) // 2, 4)

    def join(k):
        drain(fromsib.at[k], sib_r.at[k])
        mine[k] = mine[k] + fromsib[k]

    def forward(k):
        join(k)
        send(mine.at[k], yrx.at[k], y_s.at[k], y_r.at[k], {"codes": chip(k) * 2 + core})

    def mix_step(k, _):
        mix(chip(k) * 2 + 1 - core, tosib.at[k])
        send(tosib.at[k], fromsib.at[k], sib_s.at[k], sib_r.at[k], {"codes": y * 2 + 1 - core})
        mix(chip(k) * 2 + core, mine.at[k])

        @pl.when(k > 0)
        def _():
            forward(k - 1)

        return 0

    lax.fori_loop(0, 4, mix_step, 0)
    join(3)
    for k in range(3):
        drain(yrx.at[k], y_r.at[k])
    for j in range(2):
        rows = slice(j * TILE, (j + 1) * TILE)
        acc = mine[3, rows, :]
        for k in range(3):
            acc = acc + yrx[k, rows, :]
        q_out[rows, :] = acc * column(u_ref[pl.ds(2 * me_c + j, 1), :])

    drain(book.at[pl.ds(0, 60)], book_s)
    drain(cs.at[pl.ds(0, (NF - 1) * PAD)], cs_s)
    for it in range(ITERS):
        for g in range(2):
            drain(rowrx.at[it, g, pl.ds(0, NC - 1)], row_s.at[it, g])
        for stage in range(2):
            for h in range(2):
                drain(sums.at[it, stage, h, pl.ds(0, 3)], col_s.at[it, stage, h])
    for k in range(4):
        drain(tosib.at[k], sib_s.at[k])
    for k in range(3):
        drain(mine.at[k], y_s.at[k])


def per_device(target, features, codebook, tile_count, tile_cols):
    vmem = pl.BlockSpec(memory_space=pltpu.VMEM)
    smem = pl.BlockSpec(memory_space=pltpu.SMEM)
    hbm = pl.BlockSpec(memory_space=pl.ANY)
    dma = pltpu.SemaphoreType.DMA
    quantized, logs = pl.pallas_call(
        functools.partial(kernel, target),
        out_shape=(
            jax.ShapeDtypeStruct((2 * TILE, TILE), F32),
            jax.ShapeDtypeStruct((OWN, TILE), F32),
        ),
        in_specs=[hbm, hbm, smem, smem, hbm],
        out_specs=(vmem, vmem),
        scratch_shapes=[
            pltpu.VMEM((ROWS * TILE, TILE), BF16),
            pltpu.VMEM((ROWS, 1, SLOTS), jnp.int32),
            pltpu.VMEM((NF * OWN, TILE, TILE), BF16),
            pltpu.VMEM((ROWS * TILE, SLOTS * TILE), BF16),
            pltpu.VMEM((ROWS * TILE, SLOTS * TILE), F32),
            pltpu.VMEM((ROWS * TILE, TILE), F32),
            pltpu.VMEM((NF * PAD, TILE), F32),
            pltpu.VMEM((SLOTS * ROWS, NF * OWN), BF16),
            pltpu.VMEM((NF * OWN, 3 * SLOTS * ROWS), BF16),
            pltpu.VMEM((SLOTS * ROWS, TILE), F32),
            pltpu.VMEM((ITERS, 2, NC, 8, TILE), F32),
            pltpu.VMEM((ITERS, 2, 2, 4, HALF, TILE), F32),
            pltpu.VMEM((NF * OWN, TILE), F32),
            pltpu.VMEM((ROWS, TILE), F32),
            pltpu.VMEM((4, 2 * TILE, TILE), F32),
            pltpu.VMEM((4, 2 * TILE, TILE), F32),
            pltpu.VMEM((4, 2 * TILE, TILE), F32),
            pltpu.VMEM((3, 2 * TILE, TILE), F32),
            dma, dma, dma, dma, dma((2, 10, 2)), dma, dma,
            dma((ITERS, 2)), dma((ITERS, 2)), dma((ITERS, 2, 2)), dma((ITERS, 2, 2)),
            dma((4,)), dma((4,)), dma((4,)), dma((4,)),
        ],
        compiler_params=pltpu.CompilerParams(
            collective_id=0, has_side_effects=True, vmem_limit_bytes=60 * 2**20),
    )(features, codebook.reshape(OWN, TILE, TILE), tile_count.reshape(1, ROWS), tile_cols, tile_cols)
    return quantized, logs.reshape(OWN * TILE)


def solution(mesh):
    target = 32768 / 65536
    return jax.shard_map(
        functools.partial(per_device, target),
        mesh=mesh,
        in_specs=(
            P("frames", None),
            P(("codes", "frames"), None),
            P("frames", "codes"),
            P("frames", "codes", None),
        ),
        out_specs=(P(("frames", "codes"), None), P(("codes", "frames"))),
        check_vma=False,
    )
```

```python
import functools
import math

import jax
import jax.numpy as jnp
from jax import lax
from jax.experimental import pallas as pl
from jax.experimental.pallas import tpu as pltpu
from jax.sharding import PartitionSpec as P

ITERS = 4
EPS = 1e-06
INV_TEMP = 10.0
TILE = 128
SLOTS = 16
ROWS = 16
NF = 16
NC = 8
SPLIT = 5
HALF = 32
DIRECT = (2,)
OWN = 4
PAD = 8
F32 = jnp.float32
BF16 = jnp.bfloat16
NT = (((1,), (1,)), ((), ()))
MESH = pl.DeviceIdType.MESH


def tile_rows(i):
    return pl.ds(pl.multiple_of(i * TILE, TILE), TILE)


def share(p):
    return pl.ds(pl.multiple_of(p * PAD, PAD), PAD)


def column(row):
    return jnp.broadcast_to(row, (TILE, TILE)).T


def kernel(target, feat_hbm, code_hbm, cnt_s, cols_s, cols_hbm, q_out, log_out,
           feat, cols_v, book, K, exact, fs, cs, pick, place, contrib, rowrx, sums, v_ref, u_ref,
           tosib, fromsib, mine, yrx,
           feat_sem, cols_sem, code_sem, book_s, book_r, cs_s, cs_r, row_s, row_r, col_s, col_r,
           sib_s, sib_r, y_s, y_r):
    me_f = lax.axis_index("frames")
    me_c = lax.axis_index("codes")
    x, z = me_f // 4, lax.rem(me_f, 4)
    y, core = me_c // 2, lax.rem(me_c, 2)
    sub16 = lax.broadcasted_iota(jnp.int32, (ROWS, TILE), 0)
    lane = lax.broadcasted_iota(jnp.int32, (TILE, TILE), 1)
    sub8 = lax.broadcasted_iota(jnp.int32, (8, TILE), 0)
    lane16 = lax.broadcasted_iota(jnp.int32, (ROWS, TILE), 1)

    def peer_f(k):
        return lax.rem(me_f + k, NF)

    def peer_c(k):
        return lax.rem(me_c + k, NC)

    def send(src, dst, ss, rs, where):
        pltpu.make_async_remote_copy(
            src_ref=src, dst_ref=dst, send_sem=ss, recv_sem=rs,
            device_id=where, device_id_type=MESH,
        ).start()

    def drain(ref, sem):
        pltpu.make_async_copy(ref, ref, sem).wait()

    own_book = book.at[pl.ds(me_f * OWN, OWN)]
    code_copy = pltpu.make_async_copy(code_hbm, own_book, code_sem)
    code_copy.start()
    feat_copy = pltpu.make_async_copy(feat_hbm, feat, feat_sem)
    feat_copy.start()
    cols_copy = pltpu.make_async_copy(cols_hbm, cols_v, cols_sem)
    cols_copy.start()

    barrier = pltpu.get_barrier_semaphore()
    for k in range(1, NF):
        pl.semaphore_signal(barrier, inc=1, device_id={"frames": peer_f(k)}, device_id_type=MESH)
    for k in range(1, NC):
        pl.semaphore_signal(barrier, inc=1, device_id={"codes": peer_c(k)}, device_id_type=MESH)
    pl.semaphore_wait(barrier, NF - 1 + NC - 1)
    code_copy.wait()

    def at(h, first, second):
        dx, dz = (first, second) if h == 0 else (second, first)
        return lax.rem(x + dx, 4) * 4 + lax.rem(z + dz, 4)

    def chunk(h, first, second, q=None):
        base = at(h, first, second) * OWN + 2 * h
        return book.at[pl.ds(base, 2)] if q is None else book.at[pl.ds(base + q, 1)]

    def pass_on(h, stage, way, ref, first, second):
        send(ref, ref, book_s, book_r.at[h, stage, way], {"frames": at(h, first, second)})

    def first_sends(h):
        pass_on(h, 0, 0, chunk(h, 0, 0, 0), 1, 0)
        pass_on(h, 0, 1, chunk(h, 0, 0, 1), 3, 0)
        pass_on(h, 10, 0, chunk(h, 0, 0, 1), 1, 0)
        pass_on(h, 10, 1, chunk(h, 0, 0, 0), 3, 0)

    def first_forwards(h):
        drain(chunk(h, 3, 0, 0), book_r.at[h, 0, 0])
        pass_on(h, 1, 0, chunk(h, 3, 0, 0), 1, 0)
        drain(chunk(h, 1, 0, 1), book_r.at[h, 0, 1])
        pass_on(h, 1, 1, chunk(h, 1, 0, 1), 3, 0)

    def second_sends(h, j):
        pass_on(h, 2 + j, 0, chunk(h, j, 0), 0, 1)
        pass_on(h, 2 + j, 1, chunk(h, j, 0), 0, 3)
        if j in DIRECT:
            pass_on(h, 6 + j, 0, chunk(h, j, 0), 0, 2)

    def second_forwards(h, j):
        drain(chunk(h, j, 3), book_r.at[h, 2 + j, 0])
        if j not in DIRECT:
            pass_on(h, 6 + j, 0, chunk(h, j, 3, 0), 0, 1)
        drain(chunk(h, j, 1), book_r.at[h, 2 + j, 1])
        if j not in DIRECT:
            pass_on(h, 6 + j, 1, chunk(h, j, 1, 1), 0, 3)

    for h in range(2):
        first_sends(h)
    for h in range(2):
        second_sends(h, 0)

    scales = []
    for t in range(OWN):
        own = book[me_f * OWN + t].astype(F32)
        scales.append(lax.rsqrt(jnp.sum((own * own).T, axis=0, keepdims=True) / TILE + EPS))
    cs[share(me_f), :] = jnp.concatenate(scales + [jnp.ones((PAD - OWN, TILE), F32)], axis=0)
    for k in range(1, NF):
        send(cs.at[share(me_f)], cs.at[share(me_f)], cs_s, cs_r, {"frames": peer_f(k)})

    for h in range(2):
        first_forwards(h)
    for h in range(2):
        drain(chunk(h, 3, 0, 1), book_r.at[h, 10, 0])
        second_sends(h, 3)
        drain(chunk(h, 1, 0, 0), book_r.at[h, 10, 1])
        second_sends(h, 1)
    for h in range(2):
        second_forwards(h, 0)
    for h in range(2):
        drain(chunk(h, 2, 0, 0), book_r.at[h, 1, 0])
        drain(chunk(h, 2, 0, 1), book_r.at[h, 1, 1])
        second_sends(h, 2)

    feat_copy.wait()
    cols_copy.wait()

    def frame_scale(i, _):
        part = feat[tile_rows(i), :].astype(F32)
        m = jnp.sum(part * part, axis=1, keepdims=True) / TILE
        s = lax.rsqrt(m + EPS) * (INV_TEMP / TILE * math.log2(math.e))
        fs[tile_rows(i), :] = jnp.broadcast_to(s, (TILE, TILE))
        return 0

    lax.fori_loop(0, ROWS, frame_scale, 0)
    for h in range(2):
        second_forwards(h, 1)
        second_forwards(h, 3)

    count = jnp.zeros((ROWS, SLOTS), jnp.int32)
    for i in range(ROWS):
        count = jnp.where(lax.broadcasted_iota(jnp.int32, count.shape, 0) == i, cnt_s[0, i], count)
    cv = jnp.where(lax.broadcasted_iota(jnp.int32, count.shape, 1) < count, cols_v[:, 0, :], -1)
    for s in range(SLOTS):
        hot = (jnp.broadcast_to(cv[:, s:s + 1], (ROWS, TILE)) == lane16).astype(F32)
        pick[s * ROWS:(s + 1) * ROWS, :] = hot[:, :NF * OWN].astype(BF16)
        contrib[s * ROWS:(s + 1) * ROWS, :] = hot
    for h in range(2):
        turned = contrib[h * TILE:(h + 1) * TILE, :].T[:NF * OWN].astype(BF16)
        for j in range(3):
            place[:, j * 2 * TILE + h * TILE:j * 2 * TILE + (h + 1) * TILE] = turned

    for h in range(2):
        second_forwards(h, 2)
    for h in range(2):
        for j in range(4):
            if j in DIRECT:
                drain(chunk(h, j, 2), book_r.at[h, 6 + j, 0])
                continue
            drain(chunk(h, j, 2, 0), book_r.at[h, 6 + j, 0])
            drain(chunk(h, j, 2, 1), book_r.at[h, 6 + j, 1])
    drain(cs.at[pl.ds(0, (NF - 1) * PAD)], cs_r)

    def build(i, _):
        a = feat[tile_rows(i), :]
        f = fs[tile_rows(i), :]
        f = jnp.concatenate([f, f], axis=1)
        for s in range(0, SLOTS, 2):
            at2 = [cols_s[i, 0, s + j] for j in range(2)]
            words = jnp.concatenate([book[c] for c in at2], axis=0)
            scale = jnp.concatenate(
                [cs[pl.ds((c // OWN) * PAD + lax.rem(c, OWN), 1), :] for c in at2], axis=1)
            p = lax.dot_general(a, words, NT, preferred_element_type=F32)
            k = jnp.exp2(p * f * scale)
            exact[tile_rows(i), s * TILE:(s + 2) * TILE] = k
            K[tile_rows(i), s * TILE:(s + 2) * TILE] = k.astype(BF16)
        return 0

    lax.fori_loop(0, ROWS, build, 0, unroll=2)

    v_ref[...] = jnp.ones_like(v_ref)

    def hop(it, stage, h, values):
        along_x = stage == h
        slot = sums.at[it, stage, h, x if along_x else z]
        slot[...] = values
        for k in (2, 1, 3):
            where = at(0, k, 0) if along_x else at(0, 0, k)
            send(slot, slot, col_s.at[it, stage, h], col_r.at[it, stage, h], {"frames": where})

    def gathered(it, stage, h):
        drain(sums.at[it, stage, h, pl.ds(0, 3)], col_r.at[it, stage, h])
        return (sums[it, stage, h, 0] + sums[it, stage, h, 1]) + (sums[it, stage, h, 2] + sums[it, stage, h, 3])

    def sweep(it, _):
        contrib[...] = jnp.dot(pick[...], v_ref[...].astype(BF16), preferred_element_type=F32)
        V = jnp.concatenate(
            [contrib[s * ROWS:(s + 1) * ROWS, :] for s in range(SPLIT)], axis=1).astype(BF16)

        r = lax.dot_general(V, K[:, :SPLIT * TILE], NT, preferred_element_type=F32)
        side = jnp.zeros((TILE, TILE), F32)
        for g in range(2):
            for i in range(g * 8, g * 8 + 8):
                acc = jnp.zeros((TILE, TILE), F32)
                for s in range(SPLIT, SLOTS):
                    k = K[i * TILE:(i + 1) * TILE, s * TILE:(s + 1) * TILE].astype(F32)
                    acc = acc + k * contrib[s * ROWS + i:s * ROWS + i + 1, :]
                side = jnp.where(lane == i, jnp.sum(acc, axis=1, keepdims=True), side)
            total = side.T[g * 8:g * 8 + 8]
            for i in range(g * 8, g * 8 + 8):
                total = total + jnp.where(
                    sub8 == i - g * 8, r[g * 8:g * 8 + 8, i * TILE:(i + 1) * TILE], 0.0)
            slot = rowrx.at[it, g, me_c]
            slot[...] = total
            for dy, dk in ((2, 1), (2, 0), (1, 1), (3, 1), (1, 0), (3, 0), (0, 1)):
                send(slot, slot, row_s.at[it, g], row_r.at[it, g],
                     {"codes": lax.rem(y + dy, 4) * 2 + lax.rem(core + dk, 2)})
        parts = []
        for g in range(2):
            drain(rowrx.at[it, g, pl.ds(0, NC - 1)], row_r.at[it, g])
            total = rowrx[it, g, 0]
            for c in range(1, NC):
                total = total + rowrx[it, g, c]
            u = 1.0 / total
            u_ref[g * 8:g * 8 + 8, :] = u
            U = jnp.concatenate(
                [jnp.where(sub8 == i, u, 0.0) for i in range(8)], axis=1).astype(BF16)
            parts.append(jnp.dot(U, K[g * 8 * TILE:(g + 1) * 8 * TILE, :], preferred_element_type=F32))
        rest = jnp.concatenate(
            [parts[g][:, s * TILE:(s + 1) * TILE] for s in range(SLOTS) for g in range(2)], axis=0)
        hi = rest.astype(BF16)
        rest = rest - hi.astype(F32)
        mid = rest.astype(BF16)
        lo = (rest - mid.astype(F32)).astype(BF16)
        cols = jnp.dot(place[...], jnp.concatenate([hi, mid, lo], axis=0), preferred_element_type=F32)
        for h in range(2):
            hop(it, 0, h, cols[h * HALF:(h + 1) * HALF])
        for h in range(2):
            hop(it, 1, h, gathered(it, 0, h))
        csum = jnp.concatenate([gathered(it, 1, h) for h in range(2)], axis=0)
        v_ref[...] = target / csum
        return 0

    lax.fori_loop(0, ITERS, sweep, 0)
    log_out[...] = jnp.log(jnp.concatenate(
        [v_ref[pl.ds(me_f * OWN + t, 1), :] for t in range(OWN)], axis=0))

    def mix(c, dst):
        def one(j, _):
            i = 2 * c + j
            n = cnt_s[0, i]
            weights, words = [], []
            for s in range(SLOTS):
                word = cols_s[i, 0, s]
                scale = v_ref[pl.ds(word, 1), :] * jnp.where(s < n, 1.0, 0.0)
                k = exact[tile_rows(i), s * TILE:(s + 1) * TILE]
                weights.append((k * scale).astype(BF16))
                words.append(book[word])
            dst[tile_rows(j), :] = jnp.dot(
                jnp.concatenate(weights, axis=1), jnp.concatenate(words, axis=0),
                preferred_element_type=F32)
            return 0

        lax.fori_loop(0, 2, one, 0)

    def chip(k):
        return lax.rem(y + 2 + k * (k + 1) // 2, 4)

    def join(k):
        drain(fromsib.at[k], sib_r.at[k])
        mine[k] = mine[k] + fromsib[k]

    def forward(k):
        join(k)
        send(mine.at[k], yrx.at[k], y_s.at[k], y_r.at[k], {"codes": chip(k) * 2 + core})

    def mix_step(k, _):
        mix(chip(k) * 2 + 1 - core, tosib.at[k])
        send(tosib.at[k], fromsib.at[k], sib_s.at[k], sib_r.at[k], {"codes": y * 2 + 1 - core})
        mix(chip(k) * 2 + core, mine.at[k])

        @pl.when(k > 0)
        def _():
            forward(k - 1)

        return 0

    lax.fori_loop(0, 4, mix_step, 0)
    join(3)
    for k in range(3):
        drain(yrx.at[k], y_r.at[k])
    for j in range(2):
        rows = slice(j * TILE, (j + 1) * TILE)
        acc = mine[3, rows, :]
        for k in range(3):
            acc = acc + yrx[k, rows, :]
        q_out[rows, :] = acc * column(u_ref[pl.ds(2 * me_c + j, 1), :])

    drain(book.at[pl.ds(0, 60)], book_s)
    drain(cs.at[pl.ds(0, (NF - 1) * PAD)], cs_s)
    for it in range(ITERS):
        for g in range(2):
            drain(rowrx.at[it, g, pl.ds(0, NC - 1)], row_s.at[it, g])
        for stage in range(2):
            for h in range(2):
                drain(sums.at[it, stage, h, pl.ds(0, 3)], col_s.at[it, stage, h])
    for k in range(4):
        drain(tosib.at[k], sib_s.at[k])
    for k in range(3):
        drain(mine.at[k], y_s.at[k])


def per_device(target, features, codebook, tile_count, tile_cols):
    vmem = pl.BlockSpec(memory_space=pltpu.VMEM)
    smem = pl.BlockSpec(memory_space=pltpu.SMEM)
    hbm = pl.BlockSpec(memory_space=pl.ANY)
    dma = pltpu.SemaphoreType.DMA
    quantized, logs = pl.pallas_call(
        functools.partial(kernel, target),
        out_shape=(
            jax.ShapeDtypeStruct((2 * TILE, TILE), F32),
            jax.ShapeDtypeStruct((OWN, TILE), F32),
        ),
        in_specs=[hbm, hbm, smem, smem, hbm],
        out_specs=(vmem, vmem),
        scratch_shapes=[
            pltpu.VMEM((ROWS * TILE, TILE), BF16),
            pltpu.VMEM((ROWS, 1, SLOTS), jnp.int32),
            pltpu.VMEM((NF * OWN, TILE, TILE), BF16),
            pltpu.VMEM((ROWS * TILE, SLOTS * TILE), BF16),
            pltpu.VMEM((ROWS * TILE, SLOTS * TILE), F32),
            pltpu.VMEM((ROWS * TILE, TILE), F32),
            pltpu.VMEM((NF * PAD, TILE), F32),
            pltpu.VMEM((SLOTS * ROWS, NF * OWN), BF16),
            pltpu.VMEM((NF * OWN, 3 * SLOTS * ROWS), BF16),
            pltpu.VMEM((SLOTS * ROWS, TILE), F32),
            pltpu.VMEM((ITERS, 2, NC, 8, TILE), F32),
            pltpu.VMEM((ITERS, 2, 2, 4, HALF, TILE), F32),
            pltpu.VMEM((NF * OWN, TILE), F32),
            pltpu.VMEM((ROWS, TILE), F32),
            pltpu.VMEM((4, 2 * TILE, TILE), F32),
            pltpu.VMEM((4, 2 * TILE, TILE), F32),
            pltpu.VMEM((4, 2 * TILE, TILE), F32),
            pltpu.VMEM((3, 2 * TILE, TILE), F32),
            dma, dma, dma, dma, dma((2, 11, 2)), dma, dma,
            dma((ITERS, 2)), dma((ITERS, 2)), dma((ITERS, 2, 2)), dma((ITERS, 2, 2)),
            dma((4,)), dma((4,)), dma((4,)), dma((4,)),
        ],
        compiler_params=pltpu.CompilerParams(
            collective_id=0, has_side_effects=True, vmem_limit_bytes=60 * 2**20),
    )(features, codebook.reshape(OWN, TILE, TILE), tile_count.reshape(1, ROWS), tile_cols, tile_cols)
    return quantized, logs.reshape(OWN * TILE)


def solution(mesh):
    target = 32768 / 65536
    return jax.shard_map(
        functools.partial(per_device, target),
        mesh=mesh,
        in_specs=(
            P("frames", None),
            P(("codes", "frames"), None),
            P("frames", "codes"),
            P("frames", "codes", None),
        ),
        out_specs=(P(("frames", "codes"), None), P(("codes", "frames"))),
        check_vma=False,
    )
```

```python
import functools
import math

import jax
import jax.numpy as jnp
from jax import lax
from jax.experimental import pallas as pl
from jax.experimental.pallas import tpu as pltpu
from jax.sharding import PartitionSpec as P

ITERS = 4
EPS = 1e-06
INV_TEMP = 10.0
TILE = 128
SLOTS = 16
ROWS = 16
NF = 16
NC = 8
SPLIT = 5
HALF = 32
DIRECT = (2,)
OWN = 4
PAD = 8
F32 = jnp.float32
BF16 = jnp.bfloat16
NT = (((1,), (1,)), ((), ()))
MESH = pl.DeviceIdType.MESH


def tile_rows(i):
    return pl.ds(pl.multiple_of(i * TILE, TILE), TILE)


def share(p):
    return pl.ds(pl.multiple_of(p * PAD, PAD), PAD)


def column(row):
    return jnp.broadcast_to(row, (TILE, TILE)).T


def kernel(target, feat_hbm, code_hbm, cnt_s, cols_s, cols_hbm, q_out, log_out,
           feat, cols_v, book, K, exact, fs, cs, pick, place, contrib, rowrx, sums, v_ref, u_ref,
           tosib, fromsib, mine, yrx,
           feat_sem, cols_sem, code_sem, book_s, book_r, cs_s, cs_r, row_s, row_r, col_s, col_r,
           sib_s, sib_r, y_s, y_r):
    me_f = lax.axis_index("frames")
    me_c = lax.axis_index("codes")
    x, z = me_f // 4, lax.rem(me_f, 4)
    y, core = me_c // 2, lax.rem(me_c, 2)
    sub16 = lax.broadcasted_iota(jnp.int32, (ROWS, TILE), 0)
    lane = lax.broadcasted_iota(jnp.int32, (TILE, TILE), 1)
    sub8 = lax.broadcasted_iota(jnp.int32, (8, TILE), 0)
    lane16 = lax.broadcasted_iota(jnp.int32, (ROWS, TILE), 1)

    def peer_c(k):
        return lax.rem(me_c + k, NC)

    def send(src, dst, ss, rs, where):
        pltpu.make_async_remote_copy(
            src_ref=src, dst_ref=dst, send_sem=ss, recv_sem=rs,
            device_id=where, device_id_type=MESH,
        ).start()

    def drain(ref, sem):
        pltpu.make_async_copy(ref, ref, sem).wait()

    own_book = book.at[pl.ds(me_f * OWN, OWN)]
    code_copy = pltpu.make_async_copy(code_hbm, own_book, code_sem)
    code_copy.start()
    feat_copy = pltpu.make_async_copy(feat_hbm, feat, feat_sem)
    feat_copy.start()
    cols_copy = pltpu.make_async_copy(cols_hbm, cols_v, cols_sem)
    cols_copy.start()

    barrier = pltpu.get_barrier_semaphore()
    for k in (2, 1, 3):
        for where in (lax.rem(x + k, 4) * 4 + z, x * 4 + lax.rem(z + k, 4)):
            pl.semaphore_signal(barrier, inc=1, device_id={"frames": where}, device_id_type=MESH)
    for k in range(1, NC):
        pl.semaphore_signal(barrier, inc=1, device_id={"codes": peer_c(k)}, device_id_type=MESH)
    pl.semaphore_wait(barrier, 6 + NC - 1)
    code_copy.wait()

    def at(h, first, second):
        dx, dz = (first, second) if h == 0 else (second, first)
        return lax.rem(x + dx, 4) * 4 + lax.rem(z + dz, 4)

    def chunk(h, first, second, q=None):
        base = at(h, first, second) * OWN + 2 * h
        return book.at[pl.ds(base, 2)] if q is None else book.at[pl.ds(base + q, 1)]

    def pass_on(h, stage, way, ref, first, second):
        send(ref, ref, book_s, book_r.at[h, stage, way], {"frames": at(h, first, second)})

    def first_sends(h):
        pass_on(h, 0, 0, chunk(h, 0, 0, 0), 1, 0)
        pass_on(h, 0, 1, chunk(h, 0, 0, 1), 3, 0)
        pass_on(h, 10, 0, chunk(h, 0, 0, 1), 1, 0)
        pass_on(h, 10, 1, chunk(h, 0, 0, 0), 3, 0)

    def first_forwards(h):
        drain(chunk(h, 3, 0, 0), book_r.at[h, 0, 0])
        pass_on(h, 1, 0, chunk(h, 3, 0, 0), 1, 0)
        drain(chunk(h, 1, 0, 1), book_r.at[h, 0, 1])
        pass_on(h, 1, 1, chunk(h, 1, 0, 1), 3, 0)

    def second_sends(h, j):
        pass_on(h, 2 + j, 0, chunk(h, j, 0), 0, 1)
        pass_on(h, 2 + j, 1, chunk(h, j, 0), 0, 3)
        if j in DIRECT:
            pass_on(h, 6 + j, 0, chunk(h, j, 0), 0, 2)

    def second_forwards(h, j):
        drain(chunk(h, j, 3), book_r.at[h, 2 + j, 0])
        if j not in DIRECT:
            pass_on(h, 6 + j, 0, chunk(h, j, 3, 0), 0, 1)
        drain(chunk(h, j, 1), book_r.at[h, 2 + j, 1])
        if j not in DIRECT:
            pass_on(h, 6 + j, 1, chunk(h, j, 1, 1), 0, 3)

    for h in range(2):
        first_sends(h)
    for h in range(2):
        second_sends(h, 0)

    scales = []
    for t in range(OWN):
        own = book[me_f * OWN + t].astype(F32)
        scales.append(lax.rsqrt(jnp.sum((own * own).T, axis=0, keepdims=True) / TILE + EPS))
    own_cs = cs.at[share(z * 4 + x)]
    own_cs[...] = jnp.concatenate(scales + [jnp.ones((PAD - OWN, TILE), F32)], axis=0)
    for k in (2, 1, 3):
        send(own_cs, own_cs, cs_s.at[0], cs_r.at[0], {"frames": at(0, k, 0)})

    for h in range(2):
        first_forwards(h)
    for h in range(2):
        drain(chunk(h, 3, 0, 1), book_r.at[h, 10, 0])
        second_sends(h, 3)
        drain(chunk(h, 1, 0, 0), book_r.at[h, 10, 1])
        second_sends(h, 1)
    for h in range(2):
        second_forwards(h, 0)
    for h in range(2):
        drain(chunk(h, 2, 0, 0), book_r.at[h, 1, 0])
        drain(chunk(h, 2, 0, 1), book_r.at[h, 1, 1])
        second_sends(h, 2)

    feat_copy.wait()
    cols_copy.wait()

    def frame_scale(i, _):
        part = feat[tile_rows(i), :].astype(F32)
        m = jnp.sum(part * part, axis=1, keepdims=True) / TILE
        s = lax.rsqrt(m + EPS) * (INV_TEMP / TILE * math.log2(math.e))
        fs[tile_rows(i), :] = jnp.broadcast_to(s, (TILE, TILE))
        return 0

    lax.fori_loop(0, ROWS, frame_scale, 0)
    for h in range(2):
        second_forwards(h, 1)
        second_forwards(h, 3)
    drain(cs.at[pl.ds(0, 3 * PAD)], cs_r.at[0])
    line_cs = cs.at[pl.ds(pl.multiple_of(z * 4 * PAD, 4 * PAD), 4 * PAD)]
    for k in (2, 1, 3):
        send(line_cs, line_cs, cs_s.at[1], cs_r.at[1], {"frames": at(0, 0, k)})

    count = jnp.zeros((ROWS, SLOTS), jnp.int32)
    for i in range(ROWS):
        count = jnp.where(lax.broadcasted_iota(jnp.int32, count.shape, 0) == i, cnt_s[0, i], count)
    cv = jnp.where(lax.broadcasted_iota(jnp.int32, count.shape, 1) < count, cols_v[:, 0, :], -1)
    for s in range(SLOTS):
        hot = (jnp.broadcast_to(cv[:, s:s + 1], (ROWS, TILE)) == lane16).astype(F32)
        pick[s * ROWS:(s + 1) * ROWS, :] = hot[:, :NF * OWN].astype(BF16)
        contrib[s * ROWS:(s + 1) * ROWS, :] = hot
    for h in range(2):
        turned = contrib[h * TILE:(h + 1) * TILE, :].T[:NF * OWN].astype(BF16)
        for j in range(3):
            place[:, j * 2 * TILE + h * TILE:j * 2 * TILE + (h + 1) * TILE] = turned

    for h in range(2):
        second_forwards(h, 2)
    for h in range(2):
        for j in range(4):
            if j in DIRECT:
                drain(chunk(h, j, 2), book_r.at[h, 6 + j, 0])
                continue
            drain(chunk(h, j, 2, 0), book_r.at[h, 6 + j, 0])
            drain(chunk(h, j, 2, 1), book_r.at[h, 6 + j, 1])
    drain(cs.at[pl.ds(0, 3 * 4 * PAD)], cs_r.at[1])

    def scale_row(c):
        return (lax.rem(c // OWN, 4) * 4 + c // (4 * OWN)) * PAD + lax.rem(c, OWN)

    def build(i, _):
        a = feat[tile_rows(i), :]
        f = fs[tile_rows(i), :]
        f = jnp.concatenate([f, f], axis=1)
        for s in range(0, SLOTS, 2):
            at2 = [cols_s[i, 0, s + j] for j in range(2)]
            words = jnp.concatenate([book[c] for c in at2], axis=0)
            scale = jnp.concatenate(
                [cs[pl.ds(scale_row(c), 1), :] for c in at2], axis=1)
            p = lax.dot_general(a, words, NT, preferred_element_type=F32)
            k = jnp.exp2(p * f * scale)
            exact[tile_rows(i), s * TILE:(s + 2) * TILE] = k
            K[tile_rows(i), s * TILE:(s + 2) * TILE] = k.astype(BF16)
        return 0

    lax.fori_loop(0, ROWS, build, 0, unroll=2)

    v_ref[...] = jnp.ones_like(v_ref)

    def hop(it, stage, h, values):
        along_x = stage == h
        slot = sums.at[it, stage, h, x if along_x else z]
        slot[...] = values
        for k in (2, 1, 3):
            where = at(0, k, 0) if along_x else at(0, 0, k)
            send(slot, slot, col_s.at[it, stage, h], col_r.at[it, stage, h], {"frames": where})

    def gathered(it, stage, h):
        drain(sums.at[it, stage, h, pl.ds(0, 3)], col_r.at[it, stage, h])
        return (sums[it, stage, h, 0] + sums[it, stage, h, 1]) + (sums[it, stage, h, 2] + sums[it, stage, h, 3])

    def sweep(it, _):
        contrib[...] = jnp.dot(pick[...], v_ref[...].astype(BF16), preferred_element_type=F32)
        V = jnp.concatenate(
            [contrib[s * ROWS:(s + 1) * ROWS, :] for s in range(SPLIT)], axis=1).astype(BF16)

        r = lax.dot_general(V, K[:, :SPLIT * TILE], NT, preferred_element_type=F32)
        side = jnp.zeros((TILE, TILE), F32)
        for g in range(2):
            for i in range(g * 8, g * 8 + 8):
                acc = jnp.zeros((TILE, TILE), F32)
                for s in range(SPLIT, SLOTS):
                    k = K[i * TILE:(i + 1) * TILE, s * TILE:(s + 1) * TILE].astype(F32)
                    acc = acc + k * contrib[s * ROWS + i:s * ROWS + i + 1, :]
                side = jnp.where(lane == i, jnp.sum(acc, axis=1, keepdims=True), side)
            total = side.T[g * 8:g * 8 + 8]
            for i in range(g * 8, g * 8 + 8):
                total = total + jnp.where(
                    sub8 == i - g * 8, r[g * 8:g * 8 + 8, i * TILE:(i + 1) * TILE], 0.0)
            slot = rowrx.at[it, g, me_c]
            slot[...] = total
            for dy, dk in ((2, 1), (2, 0), (1, 1), (3, 1), (1, 0), (3, 0), (0, 1)):
                send(slot, slot, row_s.at[it, g], row_r.at[it, g],
                     {"codes": lax.rem(y + dy, 4) * 2 + lax.rem(core + dk, 2)})
        parts = []
        for g in range(2):
            drain(rowrx.at[it, g, pl.ds(0, NC - 1)], row_r.at[it, g])
            total = rowrx[it, g, 0]
            for c in range(1, NC):
                total = total + rowrx[it, g, c]
            u = 1.0 / total
            u_ref[g * 8:g * 8 + 8, :] = u
            U = jnp.concatenate(
                [jnp.where(sub8 == i, u, 0.0) for i in range(8)], axis=1).astype(BF16)
            parts.append(jnp.dot(U, K[g * 8 * TILE:(g + 1) * 8 * TILE, :], preferred_element_type=F32))
        rest = jnp.concatenate(
            [parts[g][:, s * TILE:(s + 1) * TILE] for s in range(SLOTS) for g in range(2)], axis=0)
        hi = rest.astype(BF16)
        rest = rest - hi.astype(F32)
        mid = rest.astype(BF16)
        lo = (rest - mid.astype(F32)).astype(BF16)
        cols = jnp.dot(place[...], jnp.concatenate([hi, mid, lo], axis=0), preferred_element_type=F32)
        for h in range(2):
            hop(it, 0, h, cols[h * HALF:(h + 1) * HALF])
        for h in range(2):
            hop(it, 1, h, gathered(it, 0, h))
        csum = jnp.concatenate([gathered(it, 1, h) for h in range(2)], axis=0)
        v_ref[...] = target / csum
        return 0

    lax.fori_loop(0, ITERS, sweep, 0)
    def mix(c, dst):
        def one(j, _):
            i = 2 * c + j
            n = cnt_s[0, i]
            weights, words = [], []
            for s in range(SLOTS):
                word = cols_s[i, 0, s]
                scale = v_ref[pl.ds(word, 1), :] * jnp.where(s < n, 1.0, 0.0)
                k = exact[tile_rows(i), s * TILE:(s + 1) * TILE]
                weights.append((k * scale).astype(BF16))
                words.append(book[word])
            dst[tile_rows(j), :] = jnp.dot(
                jnp.concatenate(weights, axis=1), jnp.concatenate(words, axis=0),
                preferred_element_type=F32)
            return 0

        lax.fori_loop(0, 2, one, 0)

    def chip(k):
        return lax.rem(y + 2 + k * (k + 1) // 2, 4)

    def join(k):
        drain(fromsib.at[k], sib_r.at[k])
        mine[k] = mine[k] + fromsib[k]

    def forward(k):
        join(k)
        send(mine.at[k], yrx.at[k], y_s.at[k], y_r.at[k], {"codes": chip(k) * 2 + core})

    def mix_step(k, _):
        mix(chip(k) * 2 + 1 - core, tosib.at[k])
        send(tosib.at[k], fromsib.at[k], sib_s.at[k], sib_r.at[k], {"codes": y * 2 + 1 - core})
        mix(chip(k) * 2 + core, mine.at[k])

        @pl.when(k > 0)
        def _():
            forward(k - 1)

        return 0

    lax.fori_loop(0, 4, mix_step, 0)
    join(3)

    drain(book.at[pl.ds(0, 60)], book_s)
    drain(cs.at[pl.ds(0, 3 * PAD)], cs_s.at[0])
    drain(cs.at[pl.ds(0, 3 * 4 * PAD)], cs_s.at[1])
    for it in range(ITERS):
        for g in range(2):
            drain(rowrx.at[it, g, pl.ds(0, NC - 1)], row_s.at[it, g])
        for stage in range(2):
            for h in range(2):
                drain(sums.at[it, stage, h, pl.ds(0, 3)], col_s.at[it, stage, h])
    for k in range(4):
        drain(tosib.at[k], sib_s.at[k])
    log_out[...] = jnp.log(jnp.concatenate(
        [v_ref[pl.ds(me_f * OWN + t, 1), :] for t in range(OWN)], axis=0))
    scale = [column(u_ref[pl.ds(2 * me_c + j, 1), :]) for j in range(2)]
    for j in range(2):
        rows = slice(j * TILE, (j + 1) * TILE)
        mine[3, rows, :] = mine[3, rows, :] * scale[j]
    for k in range(3):
        drain(yrx.at[k], y_r.at[k])
    for j in range(2):
        rows = slice(j * TILE, (j + 1) * TILE)
        acc = yrx[0, rows, :]
        for k in range(1, 3):
            acc = acc + yrx[k, rows, :]
        q_out[rows, :] = mine[3, rows, :] + acc * scale[j]

    for k in range(3):
        drain(mine.at[k], y_s.at[k])


def per_device(target, features, codebook, tile_count, tile_cols):
    vmem = pl.BlockSpec(memory_space=pltpu.VMEM)
    smem = pl.BlockSpec(memory_space=pltpu.SMEM)
    hbm = pl.BlockSpec(memory_space=pl.ANY)
    dma = pltpu.SemaphoreType.DMA
    quantized, logs = pl.pallas_call(
        functools.partial(kernel, target),
        out_shape=(
            jax.ShapeDtypeStruct((2 * TILE, TILE), F32),
            jax.ShapeDtypeStruct((OWN, TILE), F32),
        ),
        in_specs=[hbm, hbm, smem, smem, hbm],
        out_specs=(vmem, vmem),
        scratch_shapes=[
            pltpu.VMEM((ROWS * TILE, TILE), BF16),
            pltpu.VMEM((ROWS, 1, SLOTS), jnp.int32),
            pltpu.VMEM((NF * OWN, TILE, TILE), BF16),
            pltpu.VMEM((ROWS * TILE, SLOTS * TILE), BF16),
            pltpu.VMEM((ROWS * TILE, SLOTS * TILE), F32),
            pltpu.VMEM((ROWS * TILE, TILE), F32),
            pltpu.VMEM((NF * PAD, TILE), F32),
            pltpu.VMEM((SLOTS * ROWS, NF * OWN), BF16),
            pltpu.VMEM((NF * OWN, 3 * SLOTS * ROWS), BF16),
            pltpu.VMEM((SLOTS * ROWS, TILE), F32),
            pltpu.VMEM((ITERS, 2, NC, 8, TILE), F32),
            pltpu.VMEM((ITERS, 2, 2, 4, HALF, TILE), F32),
            pltpu.VMEM((NF * OWN, TILE), F32),
            pltpu.VMEM((ROWS, TILE), F32),
            pltpu.VMEM((4, 2 * TILE, TILE), F32),
            pltpu.VMEM((4, 2 * TILE, TILE), F32),
            pltpu.VMEM((4, 2 * TILE, TILE), F32),
            pltpu.VMEM((3, 2 * TILE, TILE), F32),
            dma, dma, dma, dma, dma((2, 11, 2)), dma((2,)), dma((2,)),
            dma((ITERS, 2)), dma((ITERS, 2)), dma((ITERS, 2, 2)), dma((ITERS, 2, 2)),
            dma((4,)), dma((4,)), dma((4,)), dma((4,)),
        ],
        compiler_params=pltpu.CompilerParams(
            collective_id=0, has_side_effects=True, vmem_limit_bytes=60 * 2**20),
    )(features, codebook.reshape(OWN, TILE, TILE), tile_count.reshape(1, ROWS), tile_cols, tile_cols)
    return quantized, logs.reshape(OWN * TILE)


def solution(mesh):
    target = 32768 / 65536
    return jax.shard_map(
        functools.partial(per_device, target),
        mesh=mesh,
        in_specs=(
            P("frames", None),
            P(("codes", "frames"), None),
            P("frames", "codes"),
            P("frames", "codes", None),
        ),
        out_specs=(P(("frames", "codes"), None), P(("codes", "frames"))),
        check_vma=False,
    )
```

```python
import functools
import math

import jax
import jax.numpy as jnp
from jax import lax
from jax.experimental import pallas as pl
from jax.experimental.pallas import tpu as pltpu
from jax.sharding import PartitionSpec as P

ITERS = 4
EPS = 1e-06
INV_TEMP = 10.0
TILE = 128
SLOTS = 16
ROWS = 16
NF = 16
NC = 8
SPLIT = 5
HALF = 32
DIRECT = (2,)
OWN = 4
PAD = 8
F32 = jnp.float32
BF16 = jnp.bfloat16
NT = (((1,), (1,)), ((), ()))
MESH = pl.DeviceIdType.MESH


def tile_rows(i):
    return pl.ds(pl.multiple_of(i * TILE, TILE), TILE)


def share(p):
    return pl.ds(pl.multiple_of(p * PAD, PAD), PAD)


def column(row):
    return jnp.broadcast_to(row, (TILE, TILE)).T


def kernel(target, feat_hbm, code_hbm, cnt_s, cols_s, cols_hbm, q_out, log_out,
           feat, cols_v, book, K, exact, fs, cs, pick, place, contrib, rowrx, sums, v_ref, u_ref,
           tosib, fromsib, mine, yrx,
           feat_sem, cols_sem, code_sem, book_s, book_r, cs_s, cs_r, row_s, row_r, col_s, col_r,
           sib_s, sib_r, y_s, y_r):
    me_f = lax.axis_index("frames")
    me_c = lax.axis_index("codes")
    x, z = me_f // 4, lax.rem(me_f, 4)
    y, core = me_c // 2, lax.rem(me_c, 2)
    sub16 = lax.broadcasted_iota(jnp.int32, (ROWS, TILE), 0)
    lane = lax.broadcasted_iota(jnp.int32, (TILE, TILE), 1)
    sub8 = lax.broadcasted_iota(jnp.int32, (8, TILE), 0)
    lane16 = lax.broadcasted_iota(jnp.int32, (ROWS, TILE), 1)

    def peer_c(k):
        return lax.rem(me_c + k, NC)

    def send(src, dst, ss, rs, where):
        pltpu.make_async_remote_copy(
            src_ref=src, dst_ref=dst, send_sem=ss, recv_sem=rs,
            device_id=where, device_id_type=MESH,
        ).start()

    def drain(ref, sem):
        pltpu.make_async_copy(ref, ref, sem).wait()

    own_book = book.at[pl.ds(me_f * OWN, OWN)]
    code_copy = pltpu.make_async_copy(code_hbm, own_book, code_sem)
    code_copy.start()
    feat_copy = pltpu.make_async_copy(feat_hbm, feat, feat_sem)
    feat_copy.start()
    cols_copy = pltpu.make_async_copy(cols_hbm, cols_v, cols_sem)
    cols_copy.start()

    barrier = pltpu.get_barrier_semaphore()
    for k in (2, 1, 3):
        for where in (lax.rem(x + k, 4) * 4 + z, x * 4 + lax.rem(z + k, 4)):
            pl.semaphore_signal(barrier, inc=1, device_id={"frames": where}, device_id_type=MESH)
    for k in range(1, NC):
        pl.semaphore_signal(barrier, inc=1, device_id={"codes": peer_c(k)}, device_id_type=MESH)
    pl.semaphore_wait(barrier, 6 + NC - 1)
    code_copy.wait()

    def at(h, first, second):
        dx, dz = (first, second) if h == 0 else (second, first)
        return lax.rem(x + dx, 4) * 4 + lax.rem(z + dz, 4)

    def chunk(h, first, second, q=None):
        base = at(h, first, second) * OWN + 2 * h
        return book.at[pl.ds(base, 2)] if q is None else book.at[pl.ds(base + q, 1)]

    def pass_on(h, stage, way, ref, first, second):
        send(ref, ref, book_s, book_r.at[h, stage, way], {"frames": at(h, first, second)})

    def first_sends(h):
        pass_on(h, 0, 0, chunk(h, 0, 0, 0), 1, 0)
        pass_on(h, 0, 1, chunk(h, 0, 0, 1), 3, 0)
        pass_on(h, 10, 0, chunk(h, 0, 0, 1), 1, 0)
        pass_on(h, 10, 1, chunk(h, 0, 0, 0), 3, 0)

    def first_forwards(h):
        drain(chunk(h, 3, 0, 0), book_r.at[h, 0, 0])
        pass_on(h, 1, 0, chunk(h, 3, 0, 0), 1, 0)
        drain(chunk(h, 1, 0, 1), book_r.at[h, 0, 1])
        pass_on(h, 1, 1, chunk(h, 1, 0, 1), 3, 0)

    def second_sends(h, j):
        pass_on(h, 2 + j, 0, chunk(h, j, 0), 0, 1)
        pass_on(h, 2 + j, 1, chunk(h, j, 0), 0, 3)
        if j in DIRECT:
            pass_on(h, 6 + j, 0, chunk(h, j, 0), 0, 2)

    def second_forwards(h, j):
        drain(chunk(h, j, 3), book_r.at[h, 2 + j, 0])
        if j not in DIRECT:
            pass_on(h, 6 + j, 0, chunk(h, j, 3, 0), 0, 1)
        drain(chunk(h, j, 1), book_r.at[h, 2 + j, 1])
        if j not in DIRECT:
            pass_on(h, 6 + j, 1, chunk(h, j, 1, 1), 0, 3)

    for h in range(2):
        first_sends(h)
    for h in range(2):
        second_sends(h, 0)

    scales = []
    for t in range(OWN):
        own = book[me_f * OWN + t].astype(F32)
        scales.append(lax.rsqrt(jnp.sum((own * own).T, axis=0, keepdims=True) / TILE + EPS))
    own_cs = cs.at[share(me_f)]
    own_cs[...] = jnp.concatenate(scales + [jnp.ones((PAD - OWN, TILE), F32)], axis=0)
    for k in (2, 1, 3):
        send(own_cs, own_cs, cs_s.at[0], cs_r.at[0], {"frames": at(0, 0, k)})

    for h in range(2):
        first_forwards(h)
    for h in range(2):
        drain(chunk(h, 3, 0, 1), book_r.at[h, 10, 0])
        second_sends(h, 3)
        drain(chunk(h, 1, 0, 0), book_r.at[h, 10, 1])
        second_sends(h, 1)
    for h in range(2):
        second_forwards(h, 0)
    for h in range(2):
        drain(chunk(h, 2, 0, 0), book_r.at[h, 1, 0])
        drain(chunk(h, 2, 0, 1), book_r.at[h, 1, 1])
        second_sends(h, 2)

    feat_copy.wait()
    cols_copy.wait()

    def frame_scale(i, _):
        part = feat[tile_rows(i), :].astype(F32)
        m = jnp.sum(part * part, axis=1, keepdims=True) / TILE
        s = lax.rsqrt(m + EPS) * (INV_TEMP / TILE * math.log2(math.e))
        fs[tile_rows(i), :] = jnp.broadcast_to(s, (TILE, TILE))
        return 0

    lax.fori_loop(0, ROWS, frame_scale, 0)
    for h in range(2):
        second_forwards(h, 1)
        second_forwards(h, 3)
    drain(cs.at[pl.ds(0, 3 * PAD)], cs_r.at[0])
    line_cs = cs.at[pl.ds(pl.multiple_of(x * 4 * PAD, 4 * PAD), 4 * PAD)]
    for k in (2, 1, 3):
        send(line_cs, line_cs, cs_s.at[1], cs_r.at[1], {"frames": at(0, k, 0)})

    count = jnp.zeros((ROWS, SLOTS), jnp.int32)
    for i in range(ROWS):
        count = jnp.where(lax.broadcasted_iota(jnp.int32, count.shape, 0) == i, cnt_s[0, i], count)
    cv = jnp.where(lax.broadcasted_iota(jnp.int32, count.shape, 1) < count, cols_v[:, 0, :], -1)
    for s in range(SLOTS):
        hot = (jnp.broadcast_to(cv[:, s:s + 1], (ROWS, TILE)) == lane16).astype(F32)
        pick[s * ROWS:(s + 1) * ROWS, :] = hot[:, :NF * OWN].astype(BF16)
        contrib[s * ROWS:(s + 1) * ROWS, :] = hot
    for h in range(2):
        turned = contrib[h * TILE:(h + 1) * TILE, :].T[:NF * OWN].astype(BF16)
        for j in range(3):
            place[:, j * 2 * TILE + h * TILE:j * 2 * TILE + (h + 1) * TILE] = turned

    for h in range(2):
        second_forwards(h, 2)
    for h in range(2):
        for j in range(4):
            if j in DIRECT:
                drain(chunk(h, j, 2), book_r.at[h, 6 + j, 0])
                continue
            drain(chunk(h, j, 2, 0), book_r.at[h, 6 + j, 0])
            drain(chunk(h, j, 2, 1), book_r.at[h, 6 + j, 1])
    drain(cs.at[pl.ds(0, 3 * 4 * PAD)], cs_r.at[1])

    def scale_row(c):
        return c * (PAD // OWN) - lax.rem(c, OWN)

    def build(i, _):
        a = feat[tile_rows(i), :]
        f = fs[tile_rows(i), :]
        f = jnp.concatenate([f, f], axis=1)
        for s in range(0, SLOTS, 2):
            at2 = [cols_s[i, 0, s + j] for j in range(2)]
            words = jnp.concatenate([book[c] for c in at2], axis=0)
            scale = jnp.concatenate(
                [cs[pl.ds(scale_row(c), 1), :] for c in at2], axis=1)
            p = lax.dot_general(a, words, NT, preferred_element_type=F32)
            k = jnp.exp2(p * f * scale)
            exact[tile_rows(i), s * TILE:(s + 2) * TILE] = k
            K[tile_rows(i), s * TILE:(s + 2) * TILE] = k.astype(BF16)
        return 0

    lax.fori_loop(0, ROWS, build, 0, unroll=2)

    v_ref[...] = jnp.ones_like(v_ref)

    def hop(it, stage, h, values):
        along_x = stage == h
        slot = sums.at[it, stage, h, x if along_x else z]
        slot[...] = values
        for k in (2, 1, 3):
            where = at(0, k, 0) if along_x else at(0, 0, k)
            send(slot, slot, col_s.at[it, stage, h], col_r.at[it, stage, h], {"frames": where})

    def gathered(it, stage, h):
        drain(sums.at[it, stage, h, pl.ds(0, 3)], col_r.at[it, stage, h])
        return (sums[it, stage, h, 0] + sums[it, stage, h, 1]) + (sums[it, stage, h, 2] + sums[it, stage, h, 3])

    def sweep(it, _):
        contrib[...] = jnp.dot(pick[...], v_ref[...].astype(BF16), preferred_element_type=F32)
        V = jnp.concatenate(
            [contrib[s * ROWS:(s + 1) * ROWS, :] for s in range(SPLIT)], axis=1).astype(BF16)

        r = lax.dot_general(V, K[:, :SPLIT * TILE], NT, preferred_element_type=F32)
        side = jnp.zeros((TILE, TILE), F32)
        for g in range(2):
            for i in range(g * 8, g * 8 + 8):
                acc = jnp.zeros((TILE, TILE), F32)
                for s in range(SPLIT, SLOTS):
                    k = K[i * TILE:(i + 1) * TILE, s * TILE:(s + 1) * TILE].astype(F32)
                    acc = acc + k * contrib[s * ROWS + i:s * ROWS + i + 1, :]
                side = jnp.where(lane == i, jnp.sum(acc, axis=1, keepdims=True), side)
            total = side.T[g * 8:g * 8 + 8]
            for i in range(g * 8, g * 8 + 8):
                total = total + jnp.where(
                    sub8 == i - g * 8, r[g * 8:g * 8 + 8, i * TILE:(i + 1) * TILE], 0.0)
            slot = rowrx.at[it, g, me_c]
            slot[...] = total
            for dy, dk in ((2, 1), (2, 0), (1, 1), (3, 1), (1, 0), (3, 0), (0, 1)):
                send(slot, slot, row_s.at[it, g], row_r.at[it, g],
                     {"codes": lax.rem(y + dy, 4) * 2 + lax.rem(core + dk, 2)})
        parts = []
        for g in range(2):
            drain(rowrx.at[it, g, pl.ds(0, NC - 1)], row_r.at[it, g])
            total = rowrx[it, g, 0]
            for c in range(1, NC):
                total = total + rowrx[it, g, c]
            u = 1.0 / total
            u_ref[g * 8:g * 8 + 8, :] = u
            U = jnp.concatenate(
                [jnp.where(sub8 == i, u, 0.0) for i in range(8)], axis=1).astype(BF16)
            parts.append(jnp.dot(U, K[g * 8 * TILE:(g + 1) * 8 * TILE, :], preferred_element_type=F32))
        rest = jnp.concatenate(
            [parts[g][:, s * TILE:(s + 1) * TILE] for s in range(SLOTS) for g in range(2)], axis=0)
        hi = rest.astype(BF16)
        rest = rest - hi.astype(F32)
        mid = rest.astype(BF16)
        lo = (rest - mid.astype(F32)).astype(BF16)
        cols = jnp.dot(place[...], jnp.concatenate([hi, mid, lo], axis=0), preferred_element_type=F32)
        for h in range(2):
            hop(it, 0, h, cols[h * HALF:(h + 1) * HALF])
        for h in range(2):
            hop(it, 1, h, gathered(it, 0, h))
        csum = jnp.concatenate([gathered(it, 1, h) for h in range(2)], axis=0)
        v_ref[...] = target / csum
        return 0

    lax.fori_loop(0, ITERS, sweep, 0)
    def mix(c, dst):
        def one(j, _):
            i = 2 * c + j
            n = cnt_s[0, i]
            weights, words = [], []
            for s in range(SLOTS):
                word = cols_s[i, 0, s]
                scale = v_ref[pl.ds(word, 1), :] * jnp.where(s < n, 1.0, 0.0)
                k = exact[tile_rows(i), s * TILE:(s + 1) * TILE]
                weights.append((k * scale).astype(BF16))
                words.append(book[word])
            dst[tile_rows(j), :] = jnp.dot(
                jnp.concatenate(weights, axis=1), jnp.concatenate(words, axis=0),
                preferred_element_type=F32)
            return 0

        lax.fori_loop(0, 2, one, 0)

    def chip(k):
        return lax.rem(y + 2 + k * (k + 1) // 2, 4)

    def join(k):
        drain(fromsib.at[k], sib_r.at[k])
        mine[k] = mine[k] + fromsib[k]

    def forward(k):
        join(k)
        send(mine.at[k], yrx.at[k], y_s.at[k], y_r.at[k], {"codes": chip(k) * 2 + core})

    def mix_step(k, _):
        mix(chip(k) * 2 + 1 - core, tosib.at[k])
        send(tosib.at[k], fromsib.at[k], sib_s.at[k], sib_r.at[k], {"codes": y * 2 + 1 - core})
        mix(chip(k) * 2 + core, mine.at[k])

        @pl.when(k > 0)
        def _():
            forward(k - 1)

        return 0

    lax.fori_loop(0, 4, mix_step, 0)
    join(3)

    drain(book.at[pl.ds(0, 60)], book_s)
    drain(cs.at[pl.ds(0, 3 * PAD)], cs_s.at[0])
    drain(cs.at[pl.ds(0, 3 * 4 * PAD)], cs_s.at[1])
    for it in range(ITERS):
        for g in range(2):
            drain(rowrx.at[it, g, pl.ds(0, NC - 1)], row_s.at[it, g])
        for stage in range(2):
            for h in range(2):
                drain(sums.at[it, stage, h, pl.ds(0, 3)], col_s.at[it, stage, h])
    for k in range(4):
        drain(tosib.at[k], sib_s.at[k])
    log_out[...] = jnp.log(jnp.concatenate(
        [v_ref[pl.ds(me_f * OWN + t, 1), :] for t in range(OWN)], axis=0))
    scale = [column(u_ref[pl.ds(2 * me_c + j, 1), :]) for j in range(2)]
    for j in range(2):
        rows = slice(j * TILE, (j + 1) * TILE)
        mine[3, rows, :] = mine[3, rows, :] * scale[j]
    for k in range(3):
        drain(yrx.at[k], y_r.at[k])
    for j in range(2):
        rows = slice(j * TILE, (j + 1) * TILE)
        acc = yrx[0, rows, :]
        for k in range(1, 3):
            acc = acc + yrx[k, rows, :]
        q_out[rows, :] = mine[3, rows, :] + acc * scale[j]

    for k in range(3):
        drain(mine.at[k], y_s.at[k])


def per_device(target, features, codebook, tile_count, tile_cols):
    vmem = pl.BlockSpec(memory_space=pltpu.VMEM)
    smem = pl.BlockSpec(memory_space=pltpu.SMEM)
    hbm = pl.BlockSpec(memory_space=pl.ANY)
    dma = pltpu.SemaphoreType.DMA
    quantized, logs = pl.pallas_call(
        functools.partial(kernel, target),
        out_shape=(
            jax.ShapeDtypeStruct((2 * TILE, TILE), F32),
            jax.ShapeDtypeStruct((OWN, TILE), F32),
        ),
        in_specs=[hbm, hbm, smem, smem, hbm],
        out_specs=(vmem, vmem),
        scratch_shapes=[
            pltpu.VMEM((ROWS * TILE, TILE), BF16),
            pltpu.VMEM((ROWS, 1, SLOTS), jnp.int32),
            pltpu.VMEM((NF * OWN, TILE, TILE), BF16),
            pltpu.VMEM((ROWS * TILE, SLOTS * TILE), BF16),
            pltpu.VMEM((ROWS * TILE, SLOTS * TILE), F32),
            pltpu.VMEM((ROWS * TILE, TILE), F32),
            pltpu.VMEM((NF * PAD, TILE), F32),
            pltpu.VMEM((SLOTS * ROWS, NF * OWN), BF16),
            pltpu.VMEM((NF * OWN, 3 * SLOTS * ROWS), BF16),
            pltpu.VMEM((SLOTS * ROWS, TILE), F32),
            pltpu.VMEM((ITERS, 2, NC, 8, TILE), F32),
            pltpu.VMEM((ITERS, 2, 2, 4, HALF, TILE), F32),
            pltpu.VMEM((NF * OWN, TILE), F32),
            pltpu.VMEM((ROWS, TILE), F32),
            pltpu.VMEM((4, 2 * TILE, TILE), F32),
            pltpu.VMEM((4, 2 * TILE, TILE), F32),
            pltpu.VMEM((4, 2 * TILE, TILE), F32),
            pltpu.VMEM((3, 2 * TILE, TILE), F32),
            dma, dma, dma, dma, dma((2, 11, 2)), dma((2,)), dma((2,)),
            dma((ITERS, 2)), dma((ITERS, 2)), dma((ITERS, 2, 2)), dma((ITERS, 2, 2)),
            dma((4,)), dma((4,)), dma((4,)), dma((4,)),
        ],
        compiler_params=pltpu.CompilerParams(
            collective_id=0, has_side_effects=True, vmem_limit_bytes=60 * 2**20),
    )(features, codebook.reshape(OWN, TILE, TILE), tile_count.reshape(1, ROWS), tile_cols, tile_cols)
    return quantized, logs.reshape(OWN * TILE)


def solution(mesh):
    target = 32768 / 65536
    return jax.shard_map(
        functools.partial(per_device, target),
        mesh=mesh,
        in_specs=(
            P("frames", None),
            P(("codes", "frames"), None),
            P("frames", "codes"),
            P("frames", "codes", None),
        ),
        out_specs=(P(("frames", "codes"), None), P(("codes", "frames"))),
        check_vma=False,
    )
```
